512 devices in a mesh: seq: 128 (over x, y, z_lo), head: 4 (over z_hi, core).
Axes of the slice: x: 4, y: 4, z: 16 (z_hi: 2, z_lo: 8; z = z_hi * 8 + z_lo), core: 2. Of those that a mesh axis runs over, the one named last changes fastest.
Arguments:
- tile_embed: bfloat16 [131072, 768], P('seq'), may hold values from -82 to 82
- tile_counts: int32 [2], replicated, may hold values from 32769 to 65536, as said below
- w_qkv: bfloat16 [3, 768, 768], P(None, None, 'head'), may hold values from -0.21875 to 0.21875
- w_out: bfloat16 [768, 768], replicated, may hold values from -0.21875 to 0.21875
Outputs:
- encoded: bfloat16 [131072, 768], P('seq', 'head')
The draws below stay inside these ranges and needn't reach their ends.
Inputs may be any that keep to these rules, and one draw needn't show every extreme that they name: `tile_counts`: one of the two slides holds all 65536 tiles.
All inputs are finite; a program needn't handle non-finite values.
Results may differ from the reference program's by a relative error of at most 0.007.
The reference program's roundings to bfloat16 on the way count: a program that leaves them out, or rounds other values in their place, can miss the bound.
Values may be sent and summed in bfloat16 or wider, within the bound.
A program may use at most 64 MiB of HBM per device.

```python
import jax
import jax.numpy as jnp
from jax import lax

D = 768
HEADS = 16
HD = 48
ROWS = 1024
TOKENS = 131072
LEVELS = 5


def draw_tile_embed(key, part):
    key = jax.random.fold_in(key, 5)
    first = jax.random.fold_in(key, 0)
    return jnp.clip(jax.random.normal(first, (TOKENS, D), jnp.float32), -6.0, 6.0).astype(jnp.bfloat16)


def draw_tile_counts(key, part):
    key = jax.random.fold_in(key, 7)
    first, second = jax.random.split(key)
    slide_len = TOKENS // 2
    shorter = jax.random.randint(first, (), TOKENS // 4 + 1, slide_len + 1)
    which_one = jax.random.randint(second, (), 0, 2)
    return jnp.where(jnp.arange(2) == which_one, slide_len, shorter).astype(jnp.int32)


def shard_levels(key, shape, cuts, least, top_value):
    gain = 1.0
    for dim, shards_of in cuts:
        steps = jax.random.uniform(jax.random.fold_in(jax.random.fold_in(key, 6), dim), (shards_of,), jnp.float32, least / len(cuts), top_value / len(cuts))
        gain = gain * jnp.repeat(jnp.exp(steps), shape[dim] // shards_of).reshape((-1,) + (1,) * (len(shape) - 1 - dim))
    return gain


def bell_draw(key, extent, spread, reach, cuts=(), held_as=jnp.bfloat16):
    loudness = shard_levels(key, extent, cuts, -0.22, 0.18) if cuts else 1.0
    array = jax.random.normal(key, extent, jnp.float32) * spread * loudness
    return jnp.minimum(jnp.maximum(array, -reach), reach).astype(held_as)


def setup_inputs(seed: int = 0) -> dict:
    splits = jax.random.split(jax.random.key(seed), 5)
    tile_embed = draw_tile_embed(jax.random.fold_in(splits[4], 71), 0)
    tile_counts = draw_tile_counts(jax.random.fold_in(splits[4], 71), 0)
    w_qkv = bell_draw(splits[2], (3, D, D), D ** -0.5, 0.21875, ((2, 4),))
    w_out = bell_draw(splits[3], (D, D), D ** -0.5, 0.21875)
    return {"tile_embed": tile_embed, "tile_counts": tile_counts, "w_qkv": w_qkv, "w_out": w_out}


def valid_rows(position, tile_counts, half_len):
    slide_id = position // half_len
    row_limit = jnp.where(slide_id == 0, tile_counts[0], tile_counts[1])
    return position - slide_id * half_len < row_limit


def head_terms(query_rows, key_rows, value_rows, key_ok):
    scores = jnp.dot(query_rows, key_rows.T, preferred_element_type=jnp.float32) * (query_rows.shape[1] ** -0.5)
    masked = jnp.where(key_ok[None, :], scores, -1e30)
    row_max = jnp.max(masked, axis=1)
    weights = jnp.where(key_ok[None, :], jnp.exp(scores - row_max[:, None]), 0.0)
    denom_sum = jnp.sum(weights, axis=1)
    summed = jnp.dot(weights.astype(jnp.bfloat16), value_rows, preferred_element_type=jnp.float32)
    return row_max, denom_sum, summed


def merge_state(carried, row_max, level_den, level_out):
    best, denom_sum, summed = carried
    new_best = jnp.maximum(best, row_max)
    old_wt = jnp.exp(best - new_best)
    new_wt = jnp.exp(row_max - new_best)
    return new_best, denom_sum * old_wt + level_den * new_wt, summed * old_wt[..., None] + level_out * new_wt[..., None]


def reference(tile_embed, tile_counts, w_qkv, w_out):
    projected = [jnp.dot(tile_embed, w_qkv[c], preferred_element_type=jnp.float32).astype(jnp.bfloat16).reshape(TOKENS, HEADS, HD) for c in range(3)]
    position = jnp.arange(TOKENS, dtype=jnp.int32)
    is_valid = valid_rows(position, tile_counts, TOKENS // 2)

    def one_head(head_id):
        query_all = lax.dynamic_index_in_dim(projected[0], head_id, 1, keepdims=False)
        key_all = lax.dynamic_index_in_dim(projected[1], head_id, 1, keepdims=False)
        value_all = lax.dynamic_index_in_dim(projected[2], head_id, 1, keepdims=False)
        carried = (jnp.full((TOKENS,), -1e30, jnp.float32), jnp.zeros((TOKENS,), jnp.float32), jnp.zeros((TOKENS, HD), jnp.float32))
        for tier_idx in range(LEVELS):
            stride = 2 ** tier_idx
            offset = (head_id % stride).astype(jnp.int32)

            def select_rows(source):
                shaped = source.reshape((TOKENS // stride, stride) + source.shape[1:])
                return lax.dynamic_index_in_dim(shaped, offset, 1, keepdims=False)

            seg_count = TOKENS // stride // ROWS

            def to_segments(source):
                return source.reshape((seg_count, ROWS) + source.shape[1:])

            def segment_terms(operands):
                return head_terms(operands[0], operands[1], operands[2], operands[3])

            row_max, level_den, level_out = lax.map(segment_terms, (to_segments(select_rows(query_all)), to_segments(select_rows(key_all)), to_segments(select_rows(value_all)), to_segments(select_rows(is_valid))))
            chosen = (jnp.arange(stride, dtype=jnp.int32) == offset)[None, :]
            max_full = jnp.where(chosen, row_max.reshape(-1, 1), -1e30).reshape(TOKENS)
            den_full = jnp.where(chosen, level_den.reshape(-1, 1), 0.0).reshape(TOKENS)
            out_full = jnp.where(chosen[:, :, None], level_out.reshape(-1, 1, HD), 0.0).reshape(TOKENS, HD)
            carried = merge_state(carried, max_full, den_full, out_full)
        safe_den = jnp.where(is_valid, carried[1], 1.0)
        return jnp.where(is_valid[:, None], carried[2] / safe_den[:, None], 0.0).astype(jnp.bfloat16)

    heads_out = lax.map(one_head, jnp.arange(HEADS, dtype=jnp.int32))
    attn = heads_out.transpose(1, 0, 2).reshape(TOKENS, D)
    return jnp.dot(attn, w_out, preferred_element_type=jnp.float32).astype(jnp.bfloat16)
```

```python
import functools
import math

import jax
import jax.numpy as jnp
from jax import lax
from jax.experimental import pallas as pl
from jax.experimental.pallas import tpu as pltpu
from jax.sharding import PartitionSpec as P

HD = 48
ROWS = 1024
D = 768
HALF = 64
CORD = [int(f"{j:04b}"[::-1], 2) for j in range(16)]
JOF = [CORD.index(c) for c in range(16)]
NEG = -1e30
SCALE = math.log2(math.e) / math.sqrt(HD)
MESH = pl.DeviceIdType.MESH
TILE = 256

R1, CR, FW = 8, 12, 16


def kernel(x_ref, cnt_ref, w_ref, wo_ref, o_ref, xp, wr, y, kvb, r4, qp, ka, va, acc, mx, posl, nb, att, eb,
           ss, rs, w1, w2s, w2r, cs):
    f32, bf16, i32 = jnp.float32, jnp.bfloat16, jnp.int32
    s = lax.axis_index("seq")
    hd = lax.axis_index("head")
    px, py, zl = s // 32, s // 8 % 4, s % 8
    zh, cc = hd // 2, hd % 2
    z = zh * 8 + zl
    xy = px * 4 + py
    p4 = zl % 4
    pair = p4 // 2
    inner = (p4 + 1) // 2 % 2
    za = z + 1 - 2 * (z % 2)
    zb = (z + 15 + 2 * (z % 2)) % 16
    zm = 15 - z
    ub = CR + (FW - CR) * (1 - inner)
    wb = FW - (FW - CR) * (1 - inner)

    def dev(xy_, z_, c_):
        return (xy_ * 8 + z_ % 8, z_ // 8 * 2 + c_)

    dev_a, dev_b, dev_m, dev_c = dev(xy, za, cc), dev(xy, zb, cc), dev(xy, zm, cc), dev(xy, z, 1 - cc)
    dev_y = dev(xy + 1 - 2 * (py % 2), z, cc)

    bar = pltpu.get_barrier_semaphore()
    for d in (dev_a, dev_b, dev_m, dev_c):
        pl.semaphore_signal(bar, inc=1, device_id=d, device_id_type=MESH)

    @pl.loop(1, 16)
    def _(k):
        pl.semaphore_signal(bar, inc=1, device_id=dev((xy + k) % 16, z, cc), device_id_type=MESH)

    def rcopy(src, dst, ssem, rsem, d):
        return pltpu.make_async_remote_copy(
            src_ref=src, dst_ref=dst, send_sem=ssem, recv_sem=rsem, device_id=d, device_id_type=MESH
        )

    def send_l1(g, i):
        lo, n = ((0, 1), (1, 1), (2, 2))[i]
        return rcopy(kvb.at[g, pl.ds(lo, n)], kvb.at[g, pl.ds(R1 + lo, n)], ss.at[g, i], rs.at[g, i], dev_a)

    def send_cross(g, i):
        src = (0, R1, inner + (1 - inner) * FW, inner * (R1 + 1) + (1 - inner) * (FW + 1))[i]
        return rcopy(kvb.at[g, src], kvb.at[g, CR + i], ss.at[g, 3 + i], rs.at[g, 3 + i], dev_b)

    def send_fwd(g, i):
        return rcopy(kvb.at[g, CR + i], kvb.at[g, FW + i], ss.at[g, 7 + i], rs.at[g, 7 + i], dev_a)

    def send_y(g, i):
        slot = (0, R1, ub, ub + 1, wb, wb + 1, wb + 2, wb + 3)[i]
        return rcopy(kvb.at[g, slot, pl.ds(0, 64)], r4.at[g, i], ss.at[g, 11 + i], rs.at[g, 11 + i], dev_y)

    row = lax.broadcasted_iota(i32, (ROWS, 128), 0)
    lane = lax.broadcasted_iota(i32, (ROWS, 128), 1)
    j_of = row // 64
    c_of = (j_of % 2) * 8 + (j_of // 2 % 2) * 4 + (j_of // 4 % 2) * 2 + j_of // 8
    for g in range(2):
        head = 8 * g + 4 * cc + jnp.maximum(lane - 64, 0) // 16
        posl[g] = (row % 64) * 16 + (c_of ^ head)

    rk = lax.broadcasted_iota(i32, (256, 256), 0)
    rn = lax.broadcasted_iota(i32, (256, 256), 1)
    fwd_mat = jnp.where(((rk // 16) ^ (4 * cc)) == rn % 16, jnp.where(rk % 16 == rn // 16, 1.0, 0.0), 0.0).astype(bf16)
    for q in range(4):
        t = jnp.dot(fwd_mat, x_ref[pl.ds(256 * q, 256), :], preferred_element_type=f32).astype(bf16)
        xp[:, pl.ds(16 * q, 16), :] = t.reshape(16, 16, D)

    pl.semaphore_wait(bar, 19)
    rcopy(w_ref.at[xy], wr.at[xy], w1.at[0], w1.at[1], dev_m).start()

    lane256 = lax.broadcasted_iota(i32, (1, 256), 1)
    lane_head = jnp.where(lane256 < 64, lane256 // 16, (lane256 - 64) // 48)
    q_masks = []
    for lh in range(4):
        m = jnp.where((lane256 // 48 == lh) & (lane256 < 192), 1.0, 0.0)
        q_masks.append(jnp.where(lane256 == 192 + 16 * lh, 1.0, m).astype(bf16))
    lane640 = lax.broadcasted_iota(i32, (64, 640), 1)
    head640 = lane640 % 192 // 48
    ones_lane = lane640 >= 576

    def project(g, w):
        wm = w[...].reshape(D, 640)
        for i in range(4):
            t = jnp.dot(xp[pl.ds(4 * i, 4)].reshape(256, D), wm, preferred_element_type=f32).astype(bf16)
            y[pl.ds((4 * i + 8 * g) % 16, 4)] = t.reshape(4, 64, 640)
        for j in range(16):
            c = CORD[j]
            t = y[c].astype(f32)
            for lh in range(1, 4):
                t = jnp.where(head640 == lh, y[c ^ lh].astype(f32), t)
            t = jnp.where(ones_lane, 1.0, t).astype(bf16)
            kvb[g, j // 2, pl.ds(64 * (j % 2), 64), :] = t[:, :384]
            qp[g, pl.ds(64 * j, 64), :] = t[:, 384:]

    slide = s // HALF
    count = jnp.where(slide == 0, cnt_ref[0], cnt_ref[1])

    def limit(sq):
        return count - (sq % HALF) * ROWS

    def place(g, rows, n, at, row0, sq):
        t1 = rows[:, 128:256].astype(f32)
        low = lax.broadcasted_iota(i32, (n, 128), 1) < 64
        bias = jnp.where(posl[g, pl.ds(row0, n), :] < limit(sq), 0.0, NEG)
        ka[pl.ds(at, n), 0:128] = rows[:, 0:128]
        ka[pl.ds(at, n), 128:256] = jnp.where(low, t1, bias).astype(bf16)
        va[pl.ds(at, n), 0:128] = jnp.where(low, 1.0, t1).astype(bf16)
        va[pl.ds(at, n), 128:256] = rows[:, 256:384]

    sa = s + 1 - 2 * (s % 2)
    base4 = s - s % 4
    u_src = (base4 + 2 - pair, base4 + 3 - 3 * pair)
    ob = s - zl + 4 * (1 - zl // 4)
    w_src = [ob + (3 - k) + pair * (2 * k - 3) for k in range(4)]
    to_y = 8 * (1 - 2 * (py % 2))

    def keys(g, level):
        if level == 0:
            parts = [(k, k, s) for k in range(8)]
        elif level == 1:
            parts = [(k, k, s) for k in range(4)] + [(R1 + k, k, sa) for k in range(4)]
        elif level == 2:
            parts = [(0, 0, s), (1, 1, s), (R1, 0, sa), (R1 + 1, 1, sa)]
            parts += [(ub + k, k // 2, u_src[k % 2]) for k in range(4)]
        elif level == 3:
            parts = [(0, 0, s), (R1, 0, sa), (ub, 0, u_src[0]), (ub + 1, 0, u_src[1])]
            parts += [(wb + k, 0, w_src[k]) for k in range(4)]
        else:
            srcs = [s, sa, u_src[0], u_src[1]] + w_src
            slots = [0, R1, ub, ub + 1] + [wb + k for k in range(4)]
            for i in range(8):
                place(g, kvb[g, slots[i], pl.ds(0, 64), :], 64, 64 * i, 0, srcs[i])
                place(g, r4[g, i], 64, 512 + 64 * i, 0, srcs[i] + to_y)
            return
        for i, (slot, k, sq) in enumerate(parts):
            place(g, kvb[g, slot], 128, 128 * i, 128 * k, sq)

    def attend(g, at, n, first):
        q = qp[g, pl.ds(at, n), :]
        out = jnp.zeros((n, 256), f32)
        top = jnp.zeros((n, 256), f32)
        for lh in range(4):
            sc = lax.dot_general(q * q_masks[lh], ka[...], (((1,), (1,)), ((), ())), preferred_element_type=f32)
            m = jnp.max(sc, axis=1, keepdims=True)
            wts = jnp.exp2((sc - m) * SCALE).astype(bf16)
            o = jnp.dot(wts, va[...], preferred_element_type=f32)
            out = jnp.where(lane_head == lh, o, out)
            top = jnp.where(lane_head == lh, m, top)
        if first:
            acc[g, pl.ds(at, n), :] = out
            mx[g, pl.ds(at, n), :] = top
        else:
            old = mx[g, pl.ds(at, n), :]
            new = jnp.maximum(old, top)
            a = acc[g, pl.ds(at, n), :] * jnp.exp2((old - new) * SCALE) + out * jnp.exp2((top - new) * SCALE)
            acc[g, pl.ds(at, n), :] = a
            mx[g, pl.ds(at, n), :] = new

    def when_inner(f):
        pl.when(inner == 1)(f)

    def when_outer(f):
        pl.when(inner == 0)(f)

    def phase(g, extra):
        send_l1(g, 0).start()
        send_cross(g, 0).start()
        send_l1(g, 1).start()
        keys(g, 0)

        @pl.loop(0, 4)
        def _(i):
            attend(g, pl.multiple_of(i * TILE, TILE), TILE, True)

            @pl.when(i == 0)
            def _():
                send_l1(g, 0).wait_recv()
                send_cross(g, 1).start()
                send_l1(g, 1).wait_recv()

                @when_inner
                def _():
                    send_cross(g, 2).start()
                    send_cross(g, 3).start()

                extra()

            @pl.when(i == 1)
            def _():
                @when_inner
                def _():
                    for k in range(2):
                        send_cross(g, k).wait_recv()
                        send_fwd(g, k).start()

            @pl.when(i == 2)
            def _():
                @when_outer
                def _():
                    for k in range(2):
                        send_fwd(g, k).wait_recv()
                        send_cross(g, 2 + k).start()

                send_l1(g, 2).start()

            @pl.when(i == 3)
            def _():
                @when_inner
                def _():
                    for k in range(2, 4):
                        send_cross(g, k).wait_recv()
                        send_fwd(g, k).start()

                for k in range(4):
                    send_y(g, k).start()

    def send_w(slot, k):
        return rcopy(wr.at[slot], wr.at[slot], w2s.at[k], w2r.at[slot], dev((xy + k) % 16, z, cc))

    def spread_w():
        rcopy(w_ref.at[xy], wr.at[xy], w1.at[0], w1.at[1], dev_m).wait_recv()

        @pl.loop(1, 16)
        def _(k):
            send_w(xy, k).start()

    g0, g1 = zh, 1 - zh
    project(g0, w_ref)
    phase(g0, spread_w)

    @pl.loop(1, 16)
    def _(k):
        send_w((xy + k) % 16, k).wait_recv()

    project(g1, wr)
    phase(g1, lambda: None)

    for g in range(2):
        send_l1(g, 2).wait_recv()
        keys(g, 1)

        @pl.loop(0, 2)
        def _(i):
            attend(g, pl.multiple_of(i * TILE, TILE), TILE, False)

        if g == 0:

            @when_outer
            def _():
                for gg in range(2):
                    for k in range(4):
                        send_cross(gg, k).wait_recv()
                        send_fwd(gg, k).start()
                    for k in range(2, 4):
                        send_fwd(gg, k).wait_recv()

    for g in range(2):
        keys(g, 2)
        attend(g, 0, 256, False)

    @when_inner
    def _():
        for gg in range(2):
            for k in range(4):
                send_fwd(gg, k).wait_recv()

    for gg in range(2):
        for k in range(4, 8):
            send_y(gg, k).start()
    for g in range(2):
        keys(g, 3)
        attend(g, 0, 128, False)
    for g in range(2):
        for k in range(8):
            send_y(g, k).wait_recv()
        keys(g, 4)
        attend(g, 0, 64, False)

    lim = limit(s)
    lane_t = lax.broadcasted_iota(i32, (64, 256), 1)
    hd_t = jnp.where(lane_t < 64, 4, (lane_t - 64) // 48)
    row_t = lax.broadcasted_iota(i32, (64, 256), 0)
    swap = []
    for g in range(2):

        @pl.loop(0, 16)
        def _(j):
            a = acc[g, pl.ds(pl.multiple_of(64 * j, 64), 64), :]
            den = jnp.ones((64, 256), f32)
            for lh in range(4):
                den = jnp.where(hd_t == lh, a[:, 16 * lh : 16 * lh + 1], den)
            nb[j] = jnp.where(hd_t == 4, 0.0, a / den).astype(bf16)

        for b in range(16):
            t = nb[JOF[b ^ (8 * g)]].astype(f32)
            for lh in range(1, 4):
                t = jnp.where(hd_t == lh, nb[JOF[b ^ (8 * g) ^ lh]].astype(f32), t)
            res = (b // 4 % 2 + cc) % 2 * 4 + (b - b // 4 % 2 * 4)
            att[0, g, b] = jnp.where(row_t * 16 + res < lim, t, 0.0).astype(bf16)
        cp = rcopy(att.at[0, g], att.at[1, g], cs.at[0, g], cs.at[1, g], dev_c)
        cp.start()
        swap.append(cp)

    for cp in swap:
        cp.wait_recv()
    for i in range(4):
        e = jnp.zeros((256, 192), f32)
        for g in range(2):
            own = att[0, g, pl.ds(4 * i, 4)].reshape(256, 256)
            oth = att[1, g, pl.ds(4 * (i ^ 1), 4)].reshape(256, 256)
            e += jnp.dot(own, wo_ref[2 * g + cc], preferred_element_type=f32)
            e += jnp.dot(oth, wo_ref[2 * g + 1 - cc], preferred_element_type=f32)
        eb[pl.ds(4 * i, 4)] = e.astype(bf16).reshape(4, 64, 192)
    back_mat = jnp.where(((rn // 16) ^ (4 * cc)) == rk % 16, jnp.where(rn % 16 == rk // 16, 1.0, 0.0), 0.0).astype(bf16)
    for q in range(4):
        t = eb[:, pl.ds(16 * q, 16), :].reshape(256, 192)
        o_ref[pl.ds(256 * q, 256), :] = jnp.dot(back_mat, t, preferred_element_type=f32).astype(bf16)

    rcopy(w_ref.at[xy], wr.at[xy], w1.at[0], w1.at[1], dev_m).wait_send()

    @pl.loop(1, 16)
    def _(k):
        send_w(xy, k).wait_send()

    for g in range(2):
        for k in range(3):
            send_l1(g, k).wait_send()
        for k in range(4):
            send_cross(g, k).wait_send()
            send_fwd(g, k).wait_send()
        for k in range(8):
            send_y(g, k).wait_send()
    for cp in swap:
        cp.wait_send()


def on_device(tile_embed, tile_counts, w_qkv, w_out):
    bf16, f32 = jnp.bfloat16, jnp.float32
    hd = lax.axis_index("head")
    wcat = jnp.concatenate((w_qkv[1], w_qkv[2], w_qkv[0], jnp.zeros((D, 64), bf16)), axis=1).reshape(16, 48, 640)
    cols = lax.dynamic_slice_in_dim(w_out, hd * 192, 192, 1).reshape(4, 192, 192)
    wo = jnp.pad(cols, ((0, 0), (64, 0), (0, 0)))
    vmem = pl.BlockSpec(memory_space=pltpu.VMEM)
    return pl.pallas_call(
        kernel,
        out_shape=jax.ShapeDtypeStruct((ROWS, 192), bf16),
        in_specs=[vmem, pl.BlockSpec(memory_space=pltpu.SMEM), vmem, vmem],
        out_specs=vmem,
        scratch_shapes=[
            pltpu.VMEM((16, 64, D), bf16),
            pltpu.VMEM((16, 48, 640), bf16),
            pltpu.VMEM((16, 64, 640), bf16),
            pltpu.VMEM((2, 20, 128, 384), bf16),
            pltpu.VMEM((2, 8, 64, 384), bf16),
            pltpu.VMEM((2, ROWS, 256), bf16),
            pltpu.VMEM((ROWS, 256), bf16),
            pltpu.VMEM((ROWS, 256), bf16),
            pltpu.VMEM((2, ROWS, 256), f32),
            pltpu.VMEM((2, ROWS, 256), f32),
            pltpu.VMEM((2, ROWS, 128), jnp.int32),
            pltpu.VMEM((16, 64, 256), bf16),
            pltpu.VMEM((2, 2, 16, 64, 256), bf16),
            pltpu.VMEM((16, 64, 192), bf16),
            pltpu.SemaphoreType.DMA((2, 19)),
            pltpu.SemaphoreType.DMA((2, 19)),
            pltpu.SemaphoreType.DMA((2,)),
            pltpu.SemaphoreType.DMA((16,)),
            pltpu.SemaphoreType.DMA((16,)),
            pltpu.SemaphoreType.DMA((2, 2)),
        ],
        compiler_params=pltpu.CompilerParams(
            collective_id=0, has_side_effects=True, vmem_limit_bytes=52 * 2**20
        ),
        cost_estimate=pl.CostEstimate(flops=20 * 10**9, bytes_accessed=6 * 10**6, transcendentals=17 * 10**6),
    )(tile_embed, tile_counts, wcat, wo)


def solution(mesh):
    in_specs = (P("seq", None), P(), P(None, None, "head"), P())
    out_specs = P("seq", "head")
    return jax.shard_map(
        on_device, mesh=mesh, in_specs=in_specs, out_specs=out_specs, check_vma=False
    )
```

```python
import functools
import math

import jax
import jax.numpy as jnp
from jax import lax
from jax.experimental import pallas as pl
from jax.experimental.pallas import tpu as pltpu
from jax.sharding import PartitionSpec as P

HD = 48
ROWS = 1024
D = 768
HALF = 64
CORD = [int(f"{j:04b}"[::-1], 2) for j in range(16)]
JOF = [CORD.index(c) for c in range(16)]
NEG = -1e30
SCALE = math.log2(math.e) / math.sqrt(HD)
MESH = pl.DeviceIdType.MESH
TILE = 256

R1, US, WS = 8, 12, 16


def kernel(x_ref, cnt_ref, wq_ref, wout_ref, o_ref, w_ref, wo_ref, xp, wr, y, kvb, r4, qp, ka, va, acc, mx, posl, nb, att, eb,
           ss, rs, w1, w2s, w2r, cs):
    f32, bf16, i32 = jnp.float32, jnp.bfloat16, jnp.int32
    s = lax.axis_index("seq")
    hd = lax.axis_index("head")
    px, py, zl = s // 32, s // 8 % 4, s % 8
    zh, cc = hd // 2, hd % 2
    z = zh * 8 + zl
    xy = px * 4 + py
    p4 = zl % 4
    pair = p4 // 2
    inner = (p4 + 1) // 2 % 2
    za = z + 1 - 2 * (z % 2)
    zb = (z + 15 + 2 * (z % 2)) % 16
    zw = (8 * zh + 15 - 7 * (zl // 4)) % 16
    edge = 1 - (zl + 6) // 7 + zl // 7
    zd = (8 * zh + 15 - 7 * (zl // 7)) % 16
    step = 1 - 2 * (1 - zl // 7)
    za_b = (za + 15 + 2 * (za % 2)) % 16
    zh_w = (inner * za_b + (1 - inner) * zb) // 8
    zf = z + 2 - 4 * pair

    def dev(xy_, z_, c_):
        return (xy_ * 8 + z_ % 8, z_ // 8 * 2 + c_)

    dev_a, dev_b, dev_w, dev_c = dev(xy, za, cc), dev(xy, zb, cc), dev(xy, zw, cc), dev(xy, z, 1 - cc)
    dev_f = dev(xy, zf, cc)
    dev_y = dev(xy + 1 - 2 * (py % 2), z, cc)

    bar = pltpu.get_barrier_semaphore()
    for d in (dev_a, dev_b, dev_w, dev_c, dev_f):
        pl.semaphore_signal(bar, inc=1, device_id=d, device_id_type=MESH)

    @pl.loop(1, 16)
    def _(k):
        pl.semaphore_signal(bar, inc=1, device_id=dev((xy + k) % 16, z, cc), device_id_type=MESH)

    def rcopy(src, dst, ssem, rsem, d):
        return pltpu.make_async_remote_copy(
            src_ref=src, dst_ref=dst, send_sem=ssem, recv_sem=rsem, device_id=d, device_id_type=MESH
        )

    def send_l1(g, i):
        lo, n = ((0, 1), (1, 1), (2, 2))[i]
        return rcopy(kvb.at[g, pl.ds(lo, n)], kvb.at[g, pl.ds(R1 + lo, n)], ss.at[g, i], rs.at[g, i], dev_a)

    def send_u(g, i, k):
        src, dst = ((0, US), (R1, US + 2))[i]
        return rcopy(kvb.at[g, pl.ds(src, 2)], kvb.at[g, pl.ds(dst, 2)], ss.at[g, 3 + 2 * i + k], rs.at[g, 3 + i],
                     (dev_b, dev_f)[k])

    def send_cross(g, i):
        src = (0, R1, US, US + 2)[i]
        return rcopy(kvb.at[g, src], kvb.at[g, WS + i], ss.at[g, 7 + i], rs.at[g, 7 + i], dev_b)

    def send_fwd(g, i):
        return rcopy(kvb.at[g, WS + i], kvb.at[g, WS + i], ss.at[g, 19 + i], rs.at[g, 7 + i], dev_a)

    def send_y(g, i):
        slot = (0, R1, US, US + 2, WS, WS + 1, WS + 2, WS + 3)[i]
        return rcopy(kvb.at[g, slot, pl.ds(0, 64)], r4.at[g, i], ss.at[g, 11 + i], rs.at[g, 11 + i], dev_y)

    for k in range(16):
        rows = pl.ds(48 * k, 48)
        parts = (wq_ref[1, rows, :], wq_ref[2, rows, :], wq_ref[0, rows, :], jnp.zeros((48, 64), bf16))
        w_ref[k] = jnp.concatenate(parts, axis=1)
    for k in range(4):

        @pl.when(hd == k)
        def _():
            for i in range(4):
                wo_ref[i, 0:64, :] = jnp.zeros((64, 192), bf16)
                wo_ref[i, 64:256, :] = wout_ref[pl.ds(192 * i, 192), 192 * k : 192 * k + 192]

    row = lax.broadcasted_iota(i32, (ROWS, 128), 0)
    lane = lax.broadcasted_iota(i32, (ROWS, 128), 1)
    j_of = row // 64
    c_of = (j_of % 2) * 8 + (j_of // 2 % 2) * 4 + (j_of // 4 % 2) * 2 + j_of // 8
    for g in range(2):
        head = 8 * g + 4 * cc + jnp.maximum(lane - 64, 0) // 16
        posl[g] = (row % 64) * 16 + (c_of ^ head)

    rk = lax.broadcasted_iota(i32, (256, 256), 0)
    rn = lax.broadcasted_iota(i32, (256, 256), 1)
    fwd_mat = jnp.where(((rk // 16) ^ (4 * cc)) == rn % 16, jnp.where(rk % 16 == rn // 16, 1.0, 0.0), 0.0).astype(bf16)
    for q in range(4):
        t = jnp.dot(fwd_mat, x_ref[pl.ds(256 * q, 256), :], preferred_element_type=f32).astype(bf16)
        xp[:, pl.ds(16 * q, 16), :] = t.reshape(16, 16, D)

    lane256 = lax.broadcasted_iota(i32, (1, 256), 1)
    lane_head = jnp.where(lane256 < 64, lane256 // 16, (lane256 - 64) // 48)
    q_head = jnp.where(lane256 < 192, lane256 // 48, jnp.where(lane256 % 16 == 0, (lane256 - 192) // 16, 4))
    lane640 = lax.broadcasted_iota(i32, (64, 640), 1)
    head640 = lane640 % 192 // 48
    ones_lane = lane640 >= 576

    def project(g, w, lo, n):
        wm = w[:, :, lo : lo + n].reshape(D, n)
        for i in range(4):
            t = jnp.dot(xp[pl.ds(4 * i, 4)].reshape(256, D), wm, preferred_element_type=f32).astype(bf16)
            y[pl.ds((4 * i + 8 * g) % 16, 4), :, lo : lo + n] = t.reshape(4, 64, n)
        for j in range(16):
            c = CORD[j]
            t = y[c, :, lo : lo + n].astype(f32)
            for lh in range(1, 4):
                t = jnp.where(head640[:, lo : lo + n] == lh, y[c ^ lh, :, lo : lo + n].astype(f32), t)
            if lo == 0:
                kvb[g, j // 2, pl.ds(64 * (j % 2), 64), :] = t.astype(bf16)
            else:
                t = jnp.where(ones_lane[:, lo : lo + n], 1.0, t).astype(bf16)
                qp[g, pl.ds(64 * j, 64), :] = t

    slide = s // HALF
    count = jnp.where(slide == 0, cnt_ref[0], cnt_ref[1])

    def limit(sq):
        return count - (sq % HALF) * ROWS

    def place(g, rows, n, at, row0, sq):
        t1 = rows[:, 128:256].astype(f32)
        low = lax.broadcasted_iota(i32, (n, 128), 1) < 64
        bias = jnp.where(posl[g, pl.ds(row0, n), :] < limit(sq), 0.0, NEG)
        ka[pl.ds(at, n), 0:128] = rows[:, 0:128]
        ka[pl.ds(at, n), 128:256] = jnp.where(low, t1, bias).astype(bf16)
        va[pl.ds(at, n), 0:128] = jnp.where(low, 1.0, t1).astype(bf16)
        va[pl.ds(at, n), 128:256] = rows[:, 256:384]

    sa = s + 1 - 2 * (s % 2)
    base4 = s - s % 4
    u_src = (base4 + 2 - pair, base4 + 3 - 3 * pair)
    ob = s - zl + 4 * (1 - zl // 4)
    w_src = [ob + (3 - k) + pair * (2 * k - 3) for k in range(4)]
    to_y = 8 * (1 - 2 * (py % 2))

    def keys(g, level):
        if level == 0:
            parts = [(k, k, s) for k in range(8)]
        elif level == 1:
            parts = [(k, k, s) for k in range(4)] + [(R1 + k, k, sa) for k in range(4)]
        elif level == 2:
            parts = [(0, 0, s), (1, 1, s), (R1, 0, sa), (R1 + 1, 1, sa)]
            parts += [(US + k, k % 2, u_src[k // 2]) for k in range(4)]
        elif level == 3:
            parts = [(0, 0, s), (R1, 0, sa), (US, 0, u_src[0]), (US + 2, 0, u_src[1])]
            parts += [(WS + k, 0, w_src[k]) for k in range(4)]
        else:
            srcs = [s, sa, u_src[0], u_src[1]] + w_src
            slots = [0, R1, US, US + 2] + [WS + k for k in range(4)]
            for i in range(8):
                place(g, kvb[g, slots[i], pl.ds(0, 64), :], 64, 64 * i, 0, srcs[i])
                place(g, r4[g, i], 64, 512 + 64 * i, 0, srcs[i] + to_y)
            return
        for i, (slot, k, sq) in enumerate(parts):
            place(g, kvb[g, slot], 128, 128 * i, 128 * k, sq)

    def attend(g, at, n, first):
        rows = pl.ds(at, n)
        q = qp[g, rows, :]
        out = jnp.zeros((n, 256), f32)
        top = jnp.zeros((n, 256), f32)
        for lh in range(4):
            qh = q * jnp.where(q_head == lh, 1.0, 0.0).astype(bf16)
            sc = lax.dot_general(qh, ka[...], (((1,), (1,)), ((), ())), preferred_element_type=f32)
            m = jnp.max(sc, axis=1, keepdims=True)
            wts = jnp.exp2((sc - m) * SCALE).astype(bf16)
            o = jnp.dot(wts, va[...], preferred_element_type=f32)
            out = jnp.where(lane_head == lh, o, out)
            top = jnp.where(lane_head == lh, m, top)
        if first:
            acc[g, rows, :] = out
            mx[g, rows, :] = top
        else:
            old = mx[g, rows, :]
            new = jnp.maximum(old, top)
            acc[g, rows, :] = acc[g, rows, :] * jnp.exp2((old - new) * SCALE) + out * jnp.exp2((top - new) * SCALE)
            mx[g, rows, :] = new

    def when_inner(f):
        pl.when(inner == 1)(f)

    def when_outer(f):
        pl.when(inner == 0)(f)

    def start_w(part):
        @pl.when(edge == 1)
        def _():
            @pl.loop(0, 4)
            def _(k):
                copy_w(part, k, dev(xy, (zd + k * step + 16) % 16, cc)).start()

    def copy_w(part, k, d):
        lanes = pl.ds(384 * part, 384 - 128 * part)
        return rcopy(w_ref.at[xy, :, lanes], wr.at[xy, :, lanes], w1.at[part, k], w1.at[part, 4], d)

    def send_w(part, slot, k):
        lanes = pl.ds(384 * part, 384 - 128 * part)
        ref = wr.at[slot, :, lanes]
        return rcopy(ref, ref, w2s.at[part, k], w2r.at[part, slot], dev((xy + k) % 16, z, cc))

    def spread_w(part):
        copy_w(part, 0, dev_w).wait_recv()

        @pl.loop(1, 16)
        def _(k):
            send_w(part, xy, k).start()

    def wait_w(part):
        @pl.loop(1, 16)
        def _(k):
            send_w(part, (xy + k) % 16, k).wait_recv()

    def s1(g):
        send_l1(g, 0).start()

        @when_inner
        def _():
            send_u(g, 0, 1).start()
            send_u(g, 0, 0).start()

        @when_outer
        def _():
            send_cross(g, 0).start()

        send_l1(g, 1).start()
        send_y(g, 0).start()

    def s2(g):
        send_l1(g, 0).wait_recv()
        send_l1(g, 1).wait_recv()

        @when_inner
        def _():
            send_u(g, 1, 1).start()
            send_u(g, 1, 0).start()

        @when_outer
        def _():
            send_cross(g, 1).start()

        send_l1(g, 2).start()
        send_y(g, 1).start()

    def s3(g):
        for i in range(2):
            send_u(g, i, 0).wait_recv()

            @when_outer
            def _():
                send_cross(g, 2 + i).start()

            send_y(g, 2 + i).start()

    def s4(g):
        @when_outer
        def _():
            for k in range(4):
                send_cross(g, k).wait_recv()
                send_fwd(g, k).start()
                send_y(g, 4 + k).start()


    def s5(g):
        @when_inner
        def _():
            for k in range(4):
                send_fwd(g, k).wait_recv()
                send_y(g, 4 + k).start()

    def local(g, steps):
        @pl.loop(0, 4)
        def _(i):
            attend(g, pl.multiple_of(i * TILE, TILE), TILE, True)
            for k, step in steps.items():
                pl.when(i == k)(step)

    def level(g, lv):
        keys(g, lv)
        n = ROWS >> lv

        @pl.loop(0, max(n // TILE, 1))
        def _(i):
            attend(g, pl.multiple_of(i * TILE, TILE), min(n, TILE), False)

    g0, g1 = zh, 1 - zh
    gw0, gw1 = zh_w, 1 - zh_w
    project(g0, w_ref, 0, 384)
    project(g0, w_ref, 384, 256)
    pl.semaphore_wait(bar, 19 + 4 * edge)
    start_w(0)
    s1(g0)
    start_w(1)
    keys(g0, 0)

    def step0():
        s2(g0)

    def step1():
        spread_w(0)

    def step2():
        s3(g0)
        spread_w(1)

    local(g0, {0: step0, 1: step1, 2: step2})
    wait_w(0)
    project(g1, wr, 0, 384)
    s1(g1)
    s4(gw0)
    wait_w(1)
    project(g1, wr, 384, 256)
    keys(g1, 0)

    def step4():
        s2(g1)
        s5(gw0)

    def step5():
        s3(g1)

    local(g1, {0: step4, 2: step5})
    level(g0, 2)
    s4(gw1)
    send_l1(g0, 2).wait_recv()
    level(g0, 1)
    s5(gw1)
    level(g1, 2)
    send_l1(g1, 2).wait_recv()
    level(g1, 1)
    for g in (g0, g1):
        level(g, 3)
    for g in (g0, g1):
        for k in range(8):
            send_y(g, k).wait_recv()
        level(g, 4)

    lim = limit(s)
    lane_t = lax.broadcasted_iota(i32, (64, 256), 1)
    hd_t = jnp.where(lane_t < 64, 4, (lane_t - 64) // 48)
    row_t = lax.broadcasted_iota(i32, (64, 256), 0)
    swap = []
    for g in range(2):

        @pl.loop(0, 16)
        def _(j):
            a = acc[g, pl.ds(pl.multiple_of(64 * j, 64), 64), :]
            den = jnp.ones((64, 256), f32)
            for lh in range(4):
                den = jnp.where(hd_t == lh, a[:, 16 * lh : 16 * lh + 1], den)
            nb[j] = jnp.where(hd_t == 4, 0.0, a / den).astype(bf16)

        for b in range(16):
            t = nb[JOF[b ^ (8 * g)]].astype(f32)
            for lh in range(1, 4):
                t = jnp.where(hd_t == lh, nb[JOF[b ^ (8 * g) ^ lh]].astype(f32), t)
            res = (b // 4 % 2 + cc) % 2 * 4 + (b - b // 4 % 2 * 4)
            att[0, g, b] = jnp.where(row_t * 16 + res < lim, t, 0.0).astype(bf16)
        cp = rcopy(att.at[0, g], att.at[1, g], cs.at[0, g], cs.at[1, g], dev_c)
        cp.start()
        swap.append(cp)

    for cp in swap:
        cp.wait_recv()
    for i in range(4):
        e = jnp.zeros((256, 192), f32)
        for g in range(2):
            own = att[0, g, pl.ds(4 * i, 4)].reshape(256, 256)
            oth = att[1, g, pl.ds(4 * (i ^ 1), 4)].reshape(256, 256)
            e += jnp.dot(own, wo_ref[2 * g + cc], preferred_element_type=f32)
            e += jnp.dot(oth, wo_ref[2 * g + 1 - cc], preferred_element_type=f32)
        eb[pl.ds(4 * i, 4)] = e.astype(bf16).reshape(4, 64, 192)
    back_mat = jnp.where(((rn // 16) ^ (4 * cc)) == rk % 16, jnp.where(rn % 16 == rk // 16, 1.0, 0.0), 0.0).astype(bf16)
    for q in range(4):
        t = eb[:, pl.ds(16 * q, 16), :].reshape(256, 192)
        o_ref[pl.ds(256 * q, 256), :] = jnp.dot(back_mat, t, preferred_element_type=f32).astype(bf16)

    for part in range(2):

        @pl.when(edge == 1)
        def _():
            @pl.loop(0, 4)
            def _(k):
                copy_w(part, k, dev_w).wait_send()

        @pl.loop(1, 16)
        def _(k):
            send_w(part, xy, k).wait_send()

    for g in range(2):
        for k in range(3):
            send_l1(g, k).wait_send()

        @when_inner
        def _():
            for i in range(2):
                for k in range(2):
                    send_u(g, i, k).wait_send()

        @when_outer
        def _():
            for k in range(4):
                send_cross(g, k).wait_send()
                send_fwd(g, k).wait_send()

        for k in range(8):
            send_y(g, k).wait_send()
    for cp in swap:
        cp.wait_send()


def on_device(tile_embed, tile_counts, w_qkv, w_out):
    bf16, f32 = jnp.bfloat16, jnp.float32
    vmem = pl.BlockSpec(memory_space=pltpu.VMEM)
    return pl.pallas_call(
        kernel,
        out_shape=jax.ShapeDtypeStruct((ROWS, 192), bf16),
        in_specs=[vmem, pl.BlockSpec(memory_space=pltpu.SMEM), vmem, vmem],
        out_specs=vmem,
        scratch_shapes=[
            pltpu.VMEM((16, 48, 640), bf16),
            pltpu.VMEM((4, 256, 192), bf16),
            pltpu.VMEM((16, 64, D), bf16),
            pltpu.VMEM((16, 48, 640), bf16),
            pltpu.VMEM((16, 64, 640), bf16),
            pltpu.VMEM((2, 20, 128, 384), bf16),
            pltpu.VMEM((2, 8, 64, 384), bf16),
            pltpu.VMEM((2, ROWS, 256), bf16),
            pltpu.VMEM((ROWS, 256), bf16),
            pltpu.VMEM((ROWS, 256), bf16),
            pltpu.VMEM((2, ROWS, 256), f32),
            pltpu.VMEM((2, ROWS, 256), f32),
            pltpu.VMEM((2, ROWS, 128), jnp.int32),
            pltpu.VMEM((16, 64, 256), bf16),
            pltpu.VMEM((2, 2, 16, 64, 256), bf16),
            pltpu.VMEM((16, 64, 192), bf16),
            pltpu.SemaphoreType.DMA((2, 23)),
            pltpu.SemaphoreType.DMA((2, 19)),
            pltpu.SemaphoreType.DMA((2, 5)),
            pltpu.SemaphoreType.DMA((2, 16)),
            pltpu.SemaphoreType.DMA((2, 16)),
            pltpu.SemaphoreType.DMA((2, 2)),
        ],
        compiler_params=pltpu.CompilerParams(
            collective_id=0, has_side_effects=True, vmem_limit_bytes=52 * 2**20
        ),
        cost_estimate=pl.CostEstimate(flops=20 * 10**9, bytes_accessed=6 * 10**6, transcendentals=17 * 10**6),
    )(tile_embed, tile_counts, w_qkv, w_out)


def solution(mesh):
    in_specs = (P("seq", None), P(), P(None, None, "head"), P())
    out_specs = P("seq", "head")
    return jax.shard_map(
        on_device, mesh=mesh, in_specs=in_specs, out_specs=out_specs, check_vma=False
    )
```

```python
import functools
import math

import jax
import jax.numpy as jnp
from jax import lax
from jax.experimental import pallas as pl
from jax.experimental.pallas import tpu as pltpu
from jax.sharding import PartitionSpec as P

HD = 48
ROWS = 1024
D = 768
HALF = 64
CORD = [int(f"{j:04b}"[::-1], 2) for j in range(16)]
JOF = [CORD.index(c) for c in range(16)]
NEG = -1e30
SCALE = math.log2(math.e) / math.sqrt(HD)
MESH = pl.DeviceIdType.MESH
TILE = 256

R1, US, WS = 8, 12, 16


def kernel(x_ref, cnt_ref, wq_ref, wout_ref, o_ref, w_ref, wo_ref, xp, wr, y, kvb, r4, qp, ka, va, acc, mx, posl, nb, att, eb,
           ss, rs, w1, w2s, w2r, cs):
    f32, bf16, i32 = jnp.float32, jnp.bfloat16, jnp.int32
    s = lax.axis_index("seq")
    hd = lax.axis_index("head")
    px, py, zl = s // 32, s // 8 % 4, s % 8
    zh, cc = hd // 2, hd % 2
    z = zh * 8 + zl
    xy = px * 4 + py
    p4 = zl % 4
    pair = p4 // 2
    inner = (p4 + 1) // 2 % 2
    za = z + 1 - 2 * (z % 2)
    zb = (z + 15 + 2 * (z % 2)) % 16
    zw = (8 * zh + 15 - 7 * (zl // 4)) % 16
    edge = 1 - (zl + 6) // 7 + zl // 7
    zd = (8 * zh + 15 - 7 * (zl // 7)) % 16
    step = 1 - 2 * (1 - zl // 7)
    za_b = (za + 15 + 2 * (za % 2)) % 16
    zh_w = (inner * za_b + (1 - inner) * zb) // 8
    zf = z + 2 - 4 * pair

    def dev(xy_, z_, c_):
        return (xy_ * 8 + z_ % 8, z_ // 8 * 2 + c_)

    dev_a, dev_b, dev_w, dev_c = dev(xy, za, cc), dev(xy, zb, cc), dev(xy, zw, cc), dev(xy, z, 1 - cc)
    dev_f = dev(xy, zf, cc)
    dev_y = dev(xy + 1 - 2 * (py % 2), z, cc)

    bar = pltpu.get_barrier_semaphore()
    for d in (dev_a, dev_b, dev_w, dev_c, dev_f):
        pl.semaphore_signal(bar, inc=1, device_id=d, device_id_type=MESH)

    @pl.loop(1, 16)
    def _(k):
        pl.semaphore_signal(bar, inc=1, device_id=dev((xy + k) % 16, z, cc), device_id_type=MESH)

    def rcopy(src, dst, ssem, rsem, d):
        return pltpu.make_async_remote_copy(
            src_ref=src, dst_ref=dst, send_sem=ssem, recv_sem=rsem, device_id=d, device_id_type=MESH
        )

    def send_l1(g, i):
        lo, n = ((0, 1), (1, 1), (2, 2))[i]
        return rcopy(kvb.at[g, pl.ds(lo, n)], kvb.at[g, pl.ds(R1 + lo, n)], ss.at[g, i], rs.at[g, i], dev_a)

    def send_u(g, i, k):
        src, dst = ((0, US), (R1, US + 2))[i]
        return rcopy(kvb.at[g, pl.ds(src, 2)], kvb.at[g, pl.ds(dst, 2)], ss.at[g, 3 + 2 * i + k], rs.at[g, 3 + i],
                     (dev_b, dev_f)[k])

    def send_cross(g, i):
        src = (0, R1, US, US + 2)[i]
        return rcopy(kvb.at[g, src], kvb.at[g, WS + i], ss.at[g, 7 + i], rs.at[g, 7 + i], dev_b)

    def send_fwd(g, i):
        return rcopy(kvb.at[g, WS + i], kvb.at[g, WS + i], ss.at[g, 19 + i], rs.at[g, 7 + i], dev_a)

    def send_y(g, i):
        slot = (0, R1, US, US + 2, WS, WS + 1, WS + 2, WS + 3)[i]
        return rcopy(kvb.at[g, slot, pl.ds(0, 64)], r4.at[g, i], ss.at[g, 11 + i], rs.at[g, 11 + i], dev_y)

    for k in range(16):
        rows = pl.ds(48 * k, 48)
        parts = (wq_ref[1, rows, :], wq_ref[2, rows, :], wq_ref[0, rows, :], jnp.zeros((48, 64), bf16))
        w_ref[k] = jnp.concatenate(parts, axis=1)
    for k in range(4):

        @pl.when(hd == k)
        def _():
            for i in range(4):
                wo_ref[i, 0:64, :] = jnp.zeros((64, 192), bf16)
                wo_ref[i, 64:256, :] = wout_ref[pl.ds(192 * i, 192), 192 * k : 192 * k + 192]

    row = lax.broadcasted_iota(i32, (ROWS, 128), 0)
    lane = lax.broadcasted_iota(i32, (ROWS, 128), 1)
    j_of = row // 64
    c_of = (j_of % 2) * 8 + (j_of // 2 % 2) * 4 + (j_of // 4 % 2) * 2 + j_of // 8
    for g in range(2):
        head = 8 * g + 4 * cc + jnp.maximum(lane - 64, 0) // 16
        posl[g] = (row % 64) * 16 + (c_of ^ head)

    rk = lax.broadcasted_iota(i32, (256, 256), 0)
    rn = lax.broadcasted_iota(i32, (256, 256), 1)
    fwd_mat = jnp.where(((rk // 16) ^ (4 * cc)) == rn % 16, jnp.where(rk % 16 == rn // 16, 1.0, 0.0), 0.0).astype(bf16)
    for q in range(4):
        t = jnp.dot(fwd_mat, x_ref[pl.ds(256 * q, 256), :], preferred_element_type=f32).astype(bf16)
        xp[:, pl.ds(16 * q, 16), :] = t.reshape(16, 16, D)

    lane256 = lax.broadcasted_iota(i32, (1, 256), 1)
    lane_head = jnp.where(lane256 < 64, lane256 // 16, (lane256 - 64) // 48)
    q_head = jnp.where(lane256 < 192, lane256 // 48, jnp.where(lane256 % 16 == 0, (lane256 - 192) // 16, 4))
    lane640 = lax.broadcasted_iota(i32, (64, 640), 1)
    head640 = lane640 % 192 // 48
    ones_lane = lane640 >= 576

    def project(g, w, lo, n):
        wm = w[:, :, lo : lo + n].reshape(D, n)
        for i in range(4):
            t = jnp.dot(xp[pl.ds(4 * i, 4)].reshape(256, D), wm, preferred_element_type=f32).astype(bf16)
            y[pl.ds((4 * i + 8 * g) % 16, 4), :, lo : lo + n] = t.reshape(4, 64, n)
        for j in range(16):
            c = CORD[j]
            t = y[c, :, lo : lo + n].astype(f32)
            for lh in range(1, 4):
                t = jnp.where(head640[:, lo : lo + n] == lh, y[c ^ lh, :, lo : lo + n].astype(f32), t)
            if lo == 0:
                kvb[g, j // 2, pl.ds(64 * (j % 2), 64), :] = t.astype(bf16)
            else:
                t = jnp.where(ones_lane[:, lo : lo + n], 1.0, t).astype(bf16)
                qp[g, pl.ds(64 * j, 64), :] = t

    slide = s // HALF
    count = jnp.where(slide == 0, cnt_ref[0], cnt_ref[1])

    def limit(sq):
        return count - (sq % HALF) * ROWS

    def place(g, rows, n, at, row0, sq):
        t1 = rows[:, 128:256].astype(f32)
        low = lax.broadcasted_iota(i32, (n, 128), 1) < 64
        bias = jnp.where(posl[g, pl.ds(row0, n), :] < limit(sq), 0.0, NEG)
        ka[pl.ds(at, n), 0:128] = rows[:, 0:128]
        ka[pl.ds(at, n), 128:256] = jnp.where(low, t1, bias).astype(bf16)
        va[pl.ds(at, n), 0:128] = jnp.where(low, 1.0, t1).astype(bf16)
        va[pl.ds(at, n), 128:256] = rows[:, 256:384]

    sa = s + 1 - 2 * (s % 2)
    base4 = s - s % 4
    u_src = (base4 + 2 - pair, base4 + 3 - 3 * pair)
    ob = s - zl + 4 * (1 - zl // 4)
    w_src = [ob + (3 - k) + pair * (2 * k - 3) for k in range(4)]
    to_y = 8 * (1 - 2 * (py % 2))

    def keys(g, level):
        if level == 0:
            parts = [(k, k, s) for k in range(8)]
        elif level == 1:
            parts = [(k, k, s) for k in range(4)] + [(R1 + k, k, sa) for k in range(4)]
        elif level == 2:
            parts = [(0, 0, s), (1, 1, s), (R1, 0, sa), (R1 + 1, 1, sa)]
            parts += [(US + k, k % 2, u_src[k // 2]) for k in range(4)]
        elif level == 3:
            parts = [(0, 0, s), (R1, 0, sa), (US, 0, u_src[0]), (US + 2, 0, u_src[1])]
            parts += [(WS + k, 0, w_src[k]) for k in range(4)]
        else:
            srcs = [s, sa, u_src[0], u_src[1]] + w_src
            slots = [0, R1, US, US + 2] + [WS + k for k in range(4)]
            for i in range(8):
                place(g, kvb[g, slots[i], pl.ds(0, 64), :], 64, 64 * i, 0, srcs[i])
                place(g, r4[g, i], 64, 512 + 64 * i, 0, srcs[i] + to_y)
            return
        for i, (slot, k, sq) in enumerate(parts):
            place(g, kvb[g, slot], 128, 128 * i, 128 * k, sq)

    def attend(g, at, n, first):
        rows = pl.ds(at, n)
        q = qp[g, rows, :]
        out = jnp.zeros((n, 256), f32)
        top = jnp.zeros((n, 256), f32)
        for lh in range(4):
            qh = q * jnp.where(q_head == lh, 1.0, 0.0).astype(bf16)
            sc = lax.dot_general(qh, ka[...], (((1,), (1,)), ((), ())), preferred_element_type=f32)
            m = jnp.max(sc, axis=1, keepdims=True)
            wts = jnp.exp2((sc - m) * SCALE).astype(bf16)
            o = jnp.dot(wts, va[...], preferred_element_type=f32)
            out = jnp.where(lane_head == lh, o, out)
            top = jnp.where(lane_head == lh, m, top)
        if first:
            acc[g, rows, :] = out
            mx[g, rows, :] = top
        else:
            old = mx[g, rows, :]
            new = jnp.maximum(old, top)
            acc[g, rows, :] = acc[g, rows, :] * jnp.exp2((old - new) * SCALE) + out * jnp.exp2((top - new) * SCALE)
            mx[g, rows, :] = new

    def when_inner(f):
        pl.when(inner == 1)(f)

    def when_outer(f):
        pl.when(inner == 0)(f)

    def start_w(part):
        @pl.when(edge == 1)
        def _():
            @pl.loop(0, 4)
            def _(k):
                copy_w(part, k, dev(xy, (zd + k * step + 16) % 16, cc)).start()

    def copy_w(part, k, d):
        lanes = pl.ds(384 * part, 384 - 128 * part)
        return rcopy(w_ref.at[xy, :, lanes], wr.at[xy, :, lanes], w1.at[part, k], w1.at[part, 4], d)

    def send_w(part, slot, k):
        lanes = pl.ds(384 * part, 384 - 128 * part)
        ref = wr.at[slot, :, lanes]
        return rcopy(ref, ref, w2s.at[part, k], w2r.at[part, slot], dev((xy + k) % 16, z, cc))

    def spread_w(part):
        copy_w(part, 0, dev_w).wait_recv()

        @pl.loop(1, 16)
        def _(k):
            send_w(part, xy, k).start()

    def wait_w(part):
        @pl.loop(1, 16)
        def _(k):
            send_w(part, (xy + k) % 16, k).wait_recv()

    def s1(g):
        send_l1(g, 0).start()

        @when_inner
        def _():
            send_u(g, 0, 1).start()
            send_u(g, 0, 0).start()

        @when_outer
        def _():
            send_cross(g, 0).start()

        send_l1(g, 1).start()
        send_y(g, 0).start()

    def s2(g):
        send_l1(g, 0).wait_recv()
        send_l1(g, 1).wait_recv()

        @when_inner
        def _():
            send_u(g, 1, 1).start()
            send_u(g, 1, 0).start()

        @when_outer
        def _():
            send_cross(g, 1).start()

        send_l1(g, 2).start()
        send_y(g, 1).start()

    def s3(g):
        for i in range(2):
            send_u(g, i, 0).wait_recv()

            @when_outer
            def _():
                send_cross(g, 2 + i).start()

            send_y(g, 2 + i).start()

    def s4(g):
        @when_outer
        def _():
            for k in range(4):
                send_cross(g, k).wait_recv()
                send_fwd(g, k).start()
                send_y(g, 4 + k).start()


    def s5(g):
        @when_inner
        def _():
            for k in range(4):
                send_fwd(g, k).wait_recv()
                send_y(g, 4 + k).start()

    def local(g, steps):
        @pl.loop(0, 4)
        def _(i):
            attend(g, pl.multiple_of(i * TILE, TILE), TILE, True)
            for k, step in steps.items():
                pl.when(i == k)(step)

    def level(g, lv):
        keys(g, lv)
        n = ROWS >> lv

        @pl.loop(0, max(n // TILE, 1))
        def _(i):
            attend(g, pl.multiple_of(i * TILE, TILE), min(n, TILE), False)

    g0, g1 = zh, 1 - zh
    gw0, gw1 = zh_w, 1 - zh_w
    project(g0, w_ref, 0, 384)
    project(g0, w_ref, 384, 256)
    pl.semaphore_wait(bar, 19 + 4 * edge)
    start_w(0)
    s1(g0)
    start_w(1)
    keys(g0, 0)

    def step0():
        s2(g0)
        spread_w(0)

    def step1():
        spread_w(1)

    def step2():
        s3(g0)

    local(g0, {0: step0, 1: step1, 2: step2})
    level(g0, 2)
    s4(gw0)
    wait_w(0)
    project(g1, wr, 0, 384)
    s1(g1)
    send_l1(g0, 2).wait_recv()
    keys(g0, 1)
    attend(g0, 0, 256, False)
    s2(g1)
    s5(gw0)
    attend(g0, 256, 256, False)
    wait_w(1)
    project(g1, wr, 384, 256)
    keys(g1, 0)

    def step3():
        s3(g1)

    def step4():
        s4(gw1)

    local(g1, {0: step3, 2: step4})
    level(g1, 2)
    s5(gw1)
    send_l1(g1, 2).wait_recv()
    level(g1, 1)
    for g in (g0, g1):
        level(g, 3)
    for g in (g0, g1):
        for k in range(8):
            send_y(g, k).wait_recv()
        level(g, 4)

    lim = limit(s)
    lane_t = lax.broadcasted_iota(i32, (64, 256), 1)
    hd_t = jnp.where(lane_t < 64, 4, (lane_t - 64) // 48)
    row_t = lax.broadcasted_iota(i32, (64, 256), 0)
    swap = []
    for g in range(2):

        @pl.loop(0, 16)
        def _(j):
            a = acc[g, pl.ds(pl.multiple_of(64 * j, 64), 64), :]
            den = jnp.ones((64, 256), f32)
            for lh in range(4):
                den = jnp.where(hd_t == lh, a[:, 16 * lh : 16 * lh + 1], den)
            nb[j] = jnp.where(hd_t == 4, 0.0, a / den).astype(bf16)

        for b in range(16):
            t = nb[JOF[b ^ (8 * g)]].astype(f32)
            for lh in range(1, 4):
                t = jnp.where(hd_t == lh, nb[JOF[b ^ (8 * g) ^ lh]].astype(f32), t)
            res = (b // 4 % 2 + cc) % 2 * 4 + (b - b // 4 % 2 * 4)
            att[0, g, b] = jnp.where(row_t * 16 + res < lim, t, 0.0).astype(bf16)
        cp = rcopy(att.at[0, g], att.at[1, g], cs.at[0, g], cs.at[1, g], dev_c)
        cp.start()
        swap.append(cp)

    for cp in swap:
        cp.wait_recv()
    for i in range(4):
        e = jnp.zeros((256, 192), f32)
        for g in range(2):
            own = att[0, g, pl.ds(4 * i, 4)].reshape(256, 256)
            oth = att[1, g, pl.ds(4 * (i ^ 1), 4)].reshape(256, 256)
            e += jnp.dot(own, wo_ref[2 * g + cc], preferred_element_type=f32)
            e += jnp.dot(oth, wo_ref[2 * g + 1 - cc], preferred_element_type=f32)
        eb[pl.ds(4 * i, 4)] = e.astype(bf16).reshape(4, 64, 192)
    back_mat = jnp.where(((rn // 16) ^ (4 * cc)) == rk % 16, jnp.where(rn % 16 == rk // 16, 1.0, 0.0), 0.0).astype(bf16)
    for q in range(4):
        t = eb[:, pl.ds(16 * q, 16), :].reshape(256, 192)
        o_ref[pl.ds(256 * q, 256), :] = jnp.dot(back_mat, t, preferred_element_type=f32).astype(bf16)

    for part in range(2):

        @pl.when(edge == 1)
        def _():
            @pl.loop(0, 4)
            def _(k):
                copy_w(part, k, dev_w).wait_send()

        @pl.loop(1, 16)
        def _(k):
            send_w(part, xy, k).wait_send()

    for g in range(2):
        for k in range(3):
            send_l1(g, k).wait_send()

        @when_inner
        def _():
            for i in range(2):
                for k in range(2):
                    send_u(g, i, k).wait_send()

        @when_outer
        def _():
            for k in range(4):
                send_cross(g, k).wait_send()
                send_fwd(g, k).wait_send()

        for k in range(8):
            send_y(g, k).wait_send()
    for cp in swap:
        cp.wait_send()


def on_device(tile_embed, tile_counts, w_qkv, w_out):
    bf16, f32 = jnp.bfloat16, jnp.float32
    vmem = pl.BlockSpec(memory_space=pltpu.VMEM)
    return pl.pallas_call(
        kernel,
        out_shape=jax.ShapeDtypeStruct((ROWS, 192), bf16),
        in_specs=[vmem, pl.BlockSpec(memory_space=pltpu.SMEM), vmem, vmem],
        out_specs=vmem,
        scratch_shapes=[
            pltpu.VMEM((16, 48, 640), bf16),
            pltpu.VMEM((4, 256, 192), bf16),
            pltpu.VMEM((16, 64, D), bf16),
            pltpu.VMEM((16, 48, 640), bf16),
            pltpu.VMEM((16, 64, 640), bf16),
            pltpu.VMEM((2, 20, 128, 384), bf16),
            pltpu.VMEM((2, 8, 64, 384), bf16),
            pltpu.VMEM((2, ROWS, 256), bf16),
            pltpu.VMEM((ROWS, 256), bf16),
            pltpu.VMEM((ROWS, 256), bf16),
            pltpu.VMEM((2, ROWS, 256), f32),
            pltpu.VMEM((2, ROWS, 256), f32),
            pltpu.VMEM((2, ROWS, 128), jnp.int32),
            pltpu.VMEM((16, 64, 256), bf16),
            pltpu.VMEM((2, 2, 16, 64, 256), bf16),
            pltpu.VMEM((16, 64, 192), bf16),
            pltpu.SemaphoreType.DMA((2, 23)),
            pltpu.SemaphoreType.DMA((2, 19)),
            pltpu.SemaphoreType.DMA((2, 5)),
            pltpu.SemaphoreType.DMA((2, 16)),
            pltpu.SemaphoreType.DMA((2, 16)),
            pltpu.SemaphoreType.DMA((2, 2)),
        ],
        compiler_params=pltpu.CompilerParams(
            collective_id=0, has_side_effects=True, vmem_limit_bytes=52 * 2**20
        ),
        cost_estimate=pl.CostEstimate(flops=20 * 10**9, bytes_accessed=6 * 10**6, transcendentals=17 * 10**6),
    )(tile_embed, tile_counts, w_qkv, w_out)


def solution(mesh):
    in_specs = (P("seq", None), P(), P(None, None, "head"), P())
    out_specs = P("seq", "head")
    return jax.shard_map(
        on_device, mesh=mesh, in_specs=in_specs, out_specs=out_specs, check_vma=False
    )
```

```python
import functools
import math

import jax
import jax.numpy as jnp
from jax import lax
from jax.experimental import pallas as pl
from jax.experimental.pallas import tpu as pltpu
from jax.sharding import PartitionSpec as P

HD = 48
ROWS = 1024
D = 768
HALF = 64
CORD = [int(f"{j:04b}"[::-1], 2) for j in range(16)]
JOF = [CORD.index(c) for c in range(16)]
NEG = -1e30
SCALE = math.log2(math.e) / math.sqrt(HD)
MESH = pl.DeviceIdType.MESH
TILE = 256

R1, US, WS = 8, 12, 16


def kernel(x_ref, cnt_ref, wq_ref, wout_ref, o_ref, w_ref, wo_ref, xp, wr, y, kvb, r4, qp, ka, va, acc, mx, posl, nb, att, eb,
           ss, rs, w1, w2s, w2r, cs):
    f32, bf16, i32 = jnp.float32, jnp.bfloat16, jnp.int32
    s = lax.axis_index("seq")
    hd = lax.axis_index("head")
    px, py, zl = s // 32, s // 8 % 4, s % 8
    zh, cc = hd // 2, hd % 2
    z = zh * 8 + zl
    xy = px * 4 + py
    p4 = zl % 4
    pair = p4 // 2
    inner = (p4 + 1) // 2 % 2
    za = z + 1 - 2 * (z % 2)
    zb = (z + 15 + 2 * (z % 2)) % 16
    zw = (8 * zh + 15 - 7 * (zl // 4)) % 16
    edge = 1 - (zl + 6) // 7 + zl // 7
    zd = (8 * zh + 15 - 7 * (zl // 7)) % 16
    step = 1 - 2 * (1 - zl // 7)
    za_b = (za + 15 + 2 * (za % 2)) % 16
    zh_w = (inner * za_b + (1 - inner) * zb) // 8
    zf = z + 2 - 4 * pair

    def dev(xy_, z_, c_):
        return (xy_ * 8 + z_ % 8, z_ // 8 * 2 + c_)

    dev_a, dev_b, dev_w, dev_c = dev(xy, za, cc), dev(xy, zb, cc), dev(xy, zw, cc), dev(xy, z, 1 - cc)
    dev_f = dev(xy, zf, cc)
    dev_y = dev(xy + 1 - 2 * (py % 2), z, cc)

    bar = pltpu.get_barrier_semaphore()
    for d in (dev_a, dev_b, dev_w, dev_c, dev_f):
        pl.semaphore_signal(bar, inc=1, device_id=d, device_id_type=MESH)

    @pl.loop(1, 16)
    def _(k):
        pl.semaphore_signal(bar, inc=1, device_id=dev((xy + k) % 16, z, cc), device_id_type=MESH)

    def rcopy(src, dst, ssem, rsem, d):
        return pltpu.make_async_remote_copy(
            src_ref=src, dst_ref=dst, send_sem=ssem, recv_sem=rsem, device_id=d, device_id_type=MESH
        )

    def send_l1(g, i):
        lo, n = ((0, 1), (1, 1), (2, 2))[i]
        return rcopy(kvb.at[g, pl.ds(lo, n)], kvb.at[g, pl.ds(R1 + lo, n)], ss.at[g, i], rs.at[g, i], dev_a)

    def send_u(g, i, k):
        src, dst = ((0, US), (R1, US + 2))[i]
        return rcopy(kvb.at[g, pl.ds(src, 2)], kvb.at[g, pl.ds(dst, 2)], ss.at[g, 3 + 2 * i + k], rs.at[g, 3 + i],
                     (dev_b, dev_f)[k])

    def send_cross(g, i):
        src = (0, R1, US, US + 2)[i]
        return rcopy(kvb.at[g, src], kvb.at[g, WS + i], ss.at[g, 7 + i], rs.at[g, 7 + i], dev_b)

    def send_fwd(g, i):
        return rcopy(kvb.at[g, WS + i], kvb.at[g, WS + i], ss.at[g, 19 + i], rs.at[g, 7 + i], dev_a)

    def send_y(g, i):
        slot = (0, R1, US, US + 2, WS, WS + 1, WS + 2, WS + 3)[i]
        return rcopy(kvb.at[g, slot, pl.ds(0, 64)], r4.at[g, i], ss.at[g, 11 + i], rs.at[g, 11 + i], dev_y)

    for k in range(16):
        rows = pl.ds(48 * k, 48)
        parts = (wq_ref[1, rows, :], wq_ref[2, rows, :], wq_ref[0, rows, :], jnp.zeros((48, 64), bf16))
        w_ref[k] = jnp.concatenate(parts, axis=1)
    for k in range(4):

        @pl.when(hd == k)
        def _():
            for i in range(4):
                wo_ref[i, 0:64, :] = jnp.zeros((64, 192), bf16)
                wo_ref[i, 64:256, :] = wout_ref[pl.ds(192 * i, 192), 192 * k : 192 * k + 192]

    row = lax.broadcasted_iota(i32, (ROWS, 128), 0)
    lane = lax.broadcasted_iota(i32, (ROWS, 128), 1)
    j_of = row // 64
    c_of = (j_of % 2) * 8 + (j_of // 2 % 2) * 4 + (j_of // 4 % 2) * 2 + j_of // 8
    for g in range(2):
        head = 8 * g + 4 * cc + jnp.maximum(lane - 64, 0) // 16
        posl[g] = (row % 64) * 16 + (c_of ^ head)

    rk = lax.broadcasted_iota(i32, (256, 256), 0)
    rn = lax.broadcasted_iota(i32, (256, 256), 1)
    fwd_mat = jnp.where(((rk // 16) ^ (4 * cc)) == rn % 16, jnp.where(rk % 16 == rn // 16, 1.0, 0.0), 0.0).astype(bf16)
    for q in range(4):
        t = jnp.dot(fwd_mat, x_ref[pl.ds(256 * q, 256), :], preferred_element_type=f32).astype(bf16)
        xp[:, pl.ds(16 * q, 16), :] = t.reshape(16, 16, D)

    lane256 = lax.broadcasted_iota(i32, (1, 256), 1)
    lane_head = jnp.where(lane256 < 64, lane256 // 16, (lane256 - 64) // 48)
    q_head = jnp.where(lane256 < 192, lane256 // 48, jnp.where(lane256 % 16 == 0, (lane256 - 192) // 16, 4))
    lane640 = lax.broadcasted_iota(i32, (64, 640), 1)
    head640 = lane640 % 192 // 48
    ones_lane = lane640 >= 576

    def project(g, w, lo, n):
        wm = w[:, :, lo : lo + n].reshape(D, n)
        for i in range(4):
            t = jnp.dot(xp[pl.ds(4 * i, 4)].reshape(256, D), wm, preferred_element_type=f32).astype(bf16)
            y[pl.ds((4 * i + 8 * g) % 16, 4), :, lo : lo + n] = t.reshape(4, 64, n)
        for j in range(16):
            c = CORD[j]
            t = y[c, :, lo : lo + n].astype(f32)
            for lh in range(1, 4):
                t = jnp.where(head640[:, lo : lo + n] == lh, y[c ^ lh, :, lo : lo + n].astype(f32), t)
            if lo == 0:
                kvb[g, j // 2, pl.ds(64 * (j % 2), 64), :] = t.astype(bf16)
            else:
                t = jnp.where(ones_lane[:, lo : lo + n], 1.0, t).astype(bf16)
                qp[g, pl.ds(64 * j, 64), :] = t

    slide = s // HALF
    count = jnp.where(slide == 0, cnt_ref[0], cnt_ref[1])

    def limit(sq):
        return count - (sq % HALF) * ROWS

    def place(g, rows, n, at, row0, sq):
        t1 = rows[:, 128:256].astype(f32)
        low = lax.broadcasted_iota(i32, (n, 128), 1) < 64
        bias = jnp.where(posl[g, pl.ds(row0, n), :] < limit(sq), 0.0, NEG)
        ka[pl.ds(at, n), 0:128] = rows[:, 0:128]
        ka[pl.ds(at, n), 128:256] = jnp.where(low, t1, bias).astype(bf16)
        va[pl.ds(at, n), 0:128] = jnp.where(low, 1.0, t1).astype(bf16)
        va[pl.ds(at, n), 128:256] = rows[:, 256:384]

    sa = s + 1 - 2 * (s % 2)
    base4 = s - s % 4
    u_src = (base4 + 2 - pair, base4 + 3 - 3 * pair)
    ob = s - zl + 4 * (1 - zl // 4)
    w_src = [ob + (3 - k) + pair * (2 * k - 3) for k in range(4)]
    to_y = 8 * (1 - 2 * (py % 2))

    def keys(g, level):
        if level == 0:
            parts = [(k, k, s) for k in range(8)]
        elif level == 1:
            parts = [(k, k, s) for k in range(4)] + [(R1 + k, k, sa) for k in range(4)]
        elif level == 2:
            parts = [(0, 0, s), (1, 1, s), (R1, 0, sa), (R1 + 1, 1, sa)]
            parts += [(US + k, k % 2, u_src[k // 2]) for k in range(4)]
        elif level == 3:
            parts = [(0, 0, s), (R1, 0, sa), (US, 0, u_src[0]), (US + 2, 0, u_src[1])]
            parts += [(WS + k, 0, w_src[k]) for k in range(4)]
        else:
            srcs = [s, sa, u_src[0], u_src[1]] + w_src
            slots = [0, R1, US, US + 2] + [WS + k for k in range(4)]
            for i in range(8):
                place(g, kvb[g, slots[i], pl.ds(0, 64), :], 64, 64 * i, 0, srcs[i])
                place(g, r4[g, i], 64, 512 + 64 * i, 0, srcs[i] + to_y)
            return
        for i, (slot, k, sq) in enumerate(parts):
            place(g, kvb[g, slot], 128, 128 * i, 128 * k, sq)

    def attend(g, at, n, first):
        rows = pl.ds(at, n)
        q = qp[g, rows, :]
        out = jnp.zeros((n, 256), f32)
        top = jnp.zeros((n, 256), f32)
        for lh in range(4):
            qh = q * jnp.where(q_head == lh, 1.0, 0.0).astype(bf16)
            sc = lax.dot_general(qh, ka[...], (((1,), (1,)), ((), ())), preferred_element_type=f32)
            m = jnp.max(sc, axis=1, keepdims=True)
            wts = jnp.exp2((sc - m) * SCALE).astype(bf16)
            o = jnp.dot(wts, va[...], preferred_element_type=f32)
            out = jnp.where(lane_head == lh, o, out)
            top = jnp.where(lane_head == lh, m, top)
        if first:
            acc[g, rows, :] = out
            mx[g, rows, :] = top
        else:
            old = mx[g, rows, :]
            new = jnp.maximum(old, top)
            acc[g, rows, :] = acc[g, rows, :] * jnp.exp2((old - new) * SCALE) + out * jnp.exp2((top - new) * SCALE)
            mx[g, rows, :] = new

    def when_inner(f):
        pl.when(inner == 1)(f)

    def when_outer(f):
        pl.when(inner == 0)(f)

    def start_w(part):
        @pl.when(edge == 1)
        def _():
            @pl.loop(0, 4)
            def _(k):
                copy_w(part, k, dev(xy, (zd + k * step + 16) % 16, cc)).start()

    def copy_w(part, k, d):
        lanes = pl.ds(384 * part, 384 - 128 * part)
        return rcopy(w_ref.at[xy, :, lanes], wr.at[xy, :, lanes], w1.at[part, k], w1.at[part, 4], d)

    def send_w(part, slot, k):
        lanes = pl.ds(384 * part, 384 - 128 * part)
        ref = wr.at[slot, :, lanes]
        return rcopy(ref, ref, w2s.at[part, k], w2r.at[part, slot], dev((xy + k) % 16, z, cc))

    def spread_w(part):
        copy_w(part, 0, dev_w).wait_recv()

        @pl.loop(1, 16)
        def _(k):
            send_w(part, xy, k).start()

    def wait_w(part):
        @pl.loop(1, 16)
        def _(k):
            send_w(part, (xy + k) % 16, k).wait_recv()

    def s1(g):
        send_l1(g, 0).start()

        @when_inner
        def _():
            send_u(g, 0, 1).start()
            send_u(g, 0, 0).start()

        @when_outer
        def _():
            send_cross(g, 0).start()

        send_l1(g, 1).start()
        send_y(g, 0).start()

    def s2(g):
        send_l1(g, 0).wait_recv()
        send_l1(g, 1).wait_recv()

        @when_inner
        def _():
            send_u(g, 1, 1).start()
            send_u(g, 1, 0).start()

        @when_outer
        def _():
            send_cross(g, 1).start()

        send_l1(g, 2).start()
        send_y(g, 1).start()

    def s3(g):
        for i in range(2):
            send_u(g, i, 0).wait_recv()

            @when_outer
            def _():
                send_cross(g, 2 + i).start()

            send_y(g, 2 + i).start()

    def s4(g):
        @when_outer
        def _():
            for k in range(4):
                send_cross(g, k).wait_recv()
                send_fwd(g, k).start()
                send_y(g, 4 + k).start()


    def s5(g):
        @when_inner
        def _():
            for k in range(4):
                send_fwd(g, k).wait_recv()
                send_y(g, 4 + k).start()

    def local(g, steps):
        @pl.loop(0, 4)
        def _(i):
            attend(g, pl.multiple_of(i * TILE, TILE), TILE, True)
            for k, step in steps.items():
                pl.when(i == k)(step)

    def level(g, lv):
        keys(g, lv)
        n = ROWS >> lv
        attend(g, 0, n, False)

    g0, g1 = zh, 1 - zh
    gw0, gw1 = zh_w, 1 - zh_w
    project(g0, w_ref, 0, 384)
    project(g0, w_ref, 384, 256)
    pl.semaphore_wait(bar, 19 + 4 * edge)
    start_w(0)
    s1(g0)
    start_w(1)
    keys(g0, 0)

    def step0():
        s2(g0)
        spread_w(0)

    def step1():
        spread_w(1)

    def step2():
        s3(g0)

    local(g0, {0: step0, 1: step1, 2: step2})
    level(g0, 2)
    s4(gw0)
    wait_w(0)
    project(g1, wr, 0, 384)
    s1(g1)
    send_l1(g0, 2).wait_recv()
    keys(g0, 1)
    attend(g0, 0, 256, False)
    s2(g1)
    s5(gw0)
    attend(g0, 256, 256, False)
    wait_w(1)
    project(g1, wr, 384, 256)
    keys(g1, 0)

    def step3():
        s3(g1)

    def step4():
        s4(gw1)

    local(g1, {0: step3, 2: step4})
    level(g1, 2)
    s5(gw1)
    send_l1(g1, 2).wait_recv()
    level(g1, 1)
    for g in (g0, g1):
        level(g, 3)
    for g in (g0, g1):
        for k in range(8):
            send_y(g, k).wait_recv()
        level(g, 4)

    lim = limit(s)
    lane_t = lax.broadcasted_iota(i32, (64, 256), 1)
    hd_t = jnp.where(lane_t < 64, 4, (lane_t - 64) // 48)
    row_t = lax.broadcasted_iota(i32, (64, 256), 0)
    swap = []
    for g in range(2):

        @pl.loop(0, 16)
        def _(j):
            a = acc[g, pl.ds(pl.multiple_of(64 * j, 64), 64), :]
            den = jnp.ones((64, 256), f32)
            for lh in range(4):
                den = jnp.where(hd_t == lh, a[:, 16 * lh : 16 * lh + 1], den)
            nb[j] = jnp.where(hd_t == 4, 0.0, a / den).astype(bf16)

        for b in range(16):
            t = nb[JOF[b ^ (8 * g)]].astype(f32)
            for lh in range(1, 4):
                t = jnp.where(hd_t == lh, nb[JOF[b ^ (8 * g) ^ lh]].astype(f32), t)
            res = (b // 4 % 2 + cc) % 2 * 4 + (b - b // 4 % 2 * 4)
            att[0, g, b] = jnp.where(row_t * 16 + res < lim, t, 0.0).astype(bf16)
        cp = rcopy(att.at[0, g], att.at[1, g], cs.at[0, g], cs.at[1, g], dev_c)
        cp.start()
        swap.append(cp)

    for cp in swap:
        cp.wait_recv()
    for i in range(4):
        e = jnp.zeros((256, 192), f32)
        for g in range(2):
            own = att[0, g, pl.ds(4 * i, 4)].reshape(256, 256)
            oth = att[1, g, pl.ds(4 * (i ^ 1), 4)].reshape(256, 256)
            e += jnp.dot(own, wo_ref[2 * g + cc], preferred_element_type=f32)
            e += jnp.dot(oth, wo_ref[2 * g + 1 - cc], preferred_element_type=f32)
        eb[pl.ds(4 * i, 4)] = e.astype(bf16).reshape(4, 64, 192)
    back_mat = jnp.where(((rn // 16) ^ (4 * cc)) == rk % 16, jnp.where(rn % 16 == rk // 16, 1.0, 0.0), 0.0).astype(bf16)
    for q in range(4):
        t = eb[:, pl.ds(16 * q, 16), :].reshape(256, 192)
        o_ref[pl.ds(256 * q, 256), :] = jnp.dot(back_mat, t, preferred_element_type=f32).astype(bf16)

    for part in range(2):

        @pl.when(edge == 1)
        def _():
            @pl.loop(0, 4)
            def _(k):
                copy_w(part, k, dev_w).wait_send()

        @pl.loop(1, 16)
        def _(k):
            send_w(part, xy, k).wait_send()

    for g in range(2):
        for k in range(3):
            send_l1(g, k).wait_send()

        @when_inner
        def _():
            for i in range(2):
                for k in range(2):
                    send_u(g, i, k).wait_send()

        @when_outer
        def _():
            for k in range(4):
                send_cross(g, k).wait_send()
                send_fwd(g, k).wait_send()

        for k in range(8):
            send_y(g, k).wait_send()
    for cp in swap:
        cp.wait_send()


def on_device(tile_embed, tile_counts, w_qkv, w_out):
    bf16, f32 = jnp.bfloat16, jnp.float32
    vmem = pl.BlockSpec(memory_space=pltpu.VMEM)
    return pl.pallas_call(
        kernel,
        out_shape=jax.ShapeDtypeStruct((ROWS, 192), bf16),
        in_specs=[vmem, pl.BlockSpec(memory_space=pltpu.SMEM), vmem, vmem],
        out_specs=vmem,
        scratch_shapes=[
            pltpu.VMEM((16, 48, 640), bf16),
            pltpu.VMEM((4, 256, 192), bf16),
            pltpu.VMEM((16, 64, D), bf16),
            pltpu.VMEM((16, 48, 640), bf16),
            pltpu.VMEM((16, 64, 640), bf16),
            pltpu.VMEM((2, 20, 128, 384), bf16),
            pltpu.VMEM((2, 8, 64, 384), bf16),
            pltpu.VMEM((2, ROWS, 256), bf16),
            pltpu.VMEM((ROWS, 256), bf16),
            pltpu.VMEM((ROWS, 256), bf16),
            pltpu.VMEM((2, ROWS, 256), f32),
            pltpu.VMEM((2, ROWS, 256), f32),
            pltpu.VMEM((2, ROWS, 128), jnp.int32),
            pltpu.VMEM((16, 64, 256), bf16),
            pltpu.VMEM((2, 2, 16, 64, 256), bf16),
            pltpu.VMEM((16, 64, 192), bf16),
            pltpu.SemaphoreType.DMA((2, 23)),
            pltpu.SemaphoreType.DMA((2, 19)),
            pltpu.SemaphoreType.DMA((2, 5)),
            pltpu.SemaphoreType.DMA((2, 16)),
            pltpu.SemaphoreType.DMA((2, 16)),
            pltpu.SemaphoreType.DMA((2, 2)),
        ],
        compiler_params=pltpu.CompilerParams(
            collective_id=0, has_side_effects=True, vmem_limit_bytes=52 * 2**20
        ),
        cost_estimate=pl.CostEstimate(flops=20 * 10**9, bytes_accessed=6 * 10**6, transcendentals=17 * 10**6),
    )(tile_embed, tile_counts, w_qkv, w_out)


def solution(mesh):
    in_specs = (P("seq", None), P(), P(None, None, "head"), P())
    out_specs = P("seq", "head")
    return jax.shard_map(
        on_device, mesh=mesh, in_specs=in_specs, out_specs=out_specs, check_vma=False
    )
```
